128 devices in a mesh: row: 64 (over z, y, x), mode: 2 (over core).
Axes of the slice: x: 4, y: 4, z: 4, core: 2. Of those that a mesh axis runs over, the one named last changes fastest.
Arguments:
- eigenvectors: float32 [131072, 1024], P('row', 'mode'), may hold values from -6 to 6
- reflectors: float32 [4, 131072, 256], P(None, 'row'), may hold values from -0.015625 to 0.015625
- factors: float32 [4, 256, 256], replicated, as said below
- dof_index: int32 [12, 65536], P(None, 'row'), may hold values from 0 to 131071, as said below
- stiffness: float32 [4, 12, 65536], P(None, None, 'row'), may hold values from -6 to 6
- frequency: float32 [1024], replicated, may hold values from 1 to 60
- amplitude: float32 [1024], P('mode'), may hold values from -0.2 to 0.2
- capacity: float32 [4, 65536], P(None, ('row', 'mode')), may hold values from 2 to 20
- section_ratio: float32 [65536], P(('row', 'mode')), may hold values from 0.5 to 2
Outputs:
- mode_shapes: float32 [131072, 1024], P('row', 'mode')
- demand: float32 [4, 65536], P(None, ('row', 'mode'))
- resized: float32 [65536], P(('row', 'mode'))
The draws below stay inside these ranges and needn't reach their ends.
Inputs may be any that keep to these rules, and one draw needn't show every extreme that they name: `dof_index`: every entry for member e, with d = e // 1024, lies in rows d * 2048 to d * 2048 + 2303, and every block but the last reaches that end. `factors`: upper triangular; nothing below the diagonal.
All inputs are finite; a program needn't handle non-finite values.
Results may differ from the reference program's by a relative error of at most 0.0016.
Values may be sent and summed in bfloat16 or wider, within the bound.
No kernel may reach another device: no remote copies, remote signals or barrier semaphores. Data moves between devices by JAX's collectives and lax.ppermute only.
A program may use at most 128 MiB of HBM per device.

```python
import math
import jax
import jax.numpy as jnp
from jax import lax

MODES = 1024
PANEL_COLS = 256
PANELS = 4
ROWS_DEV = 2048
HALO = 256
MEM_DEV = 1024
COMPS = 4
MEM_DOFS = 12
ROWS = 131072
MEMBERS = 65536
N_ROW = 64


def draw_factors(key, part):
    first_key = jax.random.fold_in(key, 11)
    second_key = jax.random.fold_in(key, 12)
    diagonal = jax.random.uniform(first_key, (PANELS, PANEL_COLS), jnp.float32, 1.6, 2.0)
    upper = jax.random.normal(second_key, (PANELS, PANEL_COLS, PANEL_COLS), jnp.float32) / jnp.sqrt(jnp.float32(PANEL_COLS))
    strict = jnp.triu(jnp.ones((PANEL_COLS, PANEL_COLS), jnp.float32), 1)
    identity = jnp.eye(PANEL_COLS, dtype=jnp.float32)
    return upper * strict[None] + diagonal[:, :, None] * identity[None]


def draw_dof_index(key, part):
    member = jnp.arange(MEMBERS, dtype=jnp.int32)
    block = member // MEM_DEV
    last_block = MEMBERS // MEM_DEV - 1
    upper_end = jnp.where(block == last_block, ROWS_DEV, ROWS_DEV + HALO).astype(jnp.int32)
    offsets = jax.random.randint(jax.random.fold_in(key, 21), (MEM_DOFS, MEMBERS), 0, upper_end[None, :], jnp.int32)
    entry = jnp.arange(MEM_DOFS, dtype=jnp.int32)[:, None]
    forced = jnp.logical_and(entry == 0, (member % MEM_DEV)[None, :] == 0)
    offsets = jnp.where(forced, upper_end[None, :] - 1, offsets)
    return (block * ROWS_DEV)[None, :] + offsets


def block_scale(key, extent, cuts, least, top_value):
    def one(dim, blocks):
        heights = jax.random.uniform(jax.random.fold_in(jax.random.fold_in(key, 6), dim), (blocks,), jnp.float32, least / len(cuts), top_value / len(cuts))
        return jnp.repeat(jnp.exp(heights), extent[dim] // blocks).reshape((-1,) + (1,) * (len(extent) - dim - 1))

    loudness = one(*cuts[0])
    for cut in cuts[1:]:
        loudness = loudness * one(*cut)
    return loudness


def scatter_about(rng, extent, width, reach, cuts=(), held_as=jnp.bfloat16):
    array = width * jax.random.normal(rng, extent, jnp.float32)
    if cuts:
        array = array * block_scale(rng, extent, cuts, -0.22, 0.18)
    return jnp.clip(array, -reach, reach).astype(held_as)


def setup_inputs(seed: int = 0) -> dict:
    key_of = jax.random.split(jax.random.key(seed), 10)
    return {
        "eigenvectors": scatter_about(key_of[0], (ROWS, MODES), 1.0, 6.0, ((0, 64), (1, 2)), jnp.float32),
        "reflectors": scatter_about(key_of[1], (PANELS, ROWS, PANEL_COLS), ROWS ** -0.5, 0.015625, ((1, 64),), jnp.float32),
        "factors": draw_factors(jax.random.fold_in(key_of[9], 71), 0),
        "dof_index": draw_dof_index(jax.random.fold_in(key_of[9], 71), 0),
        "stiffness": scatter_about(key_of[4], (COMPS, MEM_DOFS, MEMBERS), 1.0, 6.0, ((2, 64),), jnp.float32),
        "frequency": jnp.clip(jnp.exp(jax.random.uniform(key_of[5], (MODES,), jnp.float32, math.log(1.0), math.log(60.0))), 1.0, 60.0),
        "amplitude": scatter_about(key_of[6], (MODES,), 0.03125, 0.2, ((0, 2),), jnp.float32),
        "capacity": jnp.clip(jnp.exp(math.log(20.0) - 2.3025851 * jax.random.uniform(key_of[7], (COMPS, MEMBERS), jnp.float32) ** block_scale(key_of[7], (COMPS, MEMBERS), ((1, 128),), -0.2, 0.2)), 2.0, 20.0),
        "section_ratio": jnp.clip(jnp.exp(math.log(2.0) - 1.3862944 * jax.random.uniform(key_of[8], (MEMBERS,), jnp.float32) ** block_scale(key_of[8], (MEMBERS,), ((0, 128),), -0.2, 0.2)), 0.5, 2.0),
    }


damping_ratio = 0.05

def correlation(frequency):
    freq_ratio = frequency[None, :] / frequency[:, None]
    squared = damping_ratio * damping_ratio
    numerator = 8.0 * squared * (1.0 + freq_ratio) * freq_ratio * jnp.sqrt(freq_ratio)
    denominator = (1.0 - freq_ratio * freq_ratio) ** 2 + 4.0 * squared * freq_ratio * (1.0 + freq_ratio) ** 2
    return (numerator / denominator).astype(jnp.bfloat16)

def reference(eigenvectors, reflectors, factors, dof_index, stiffness, frequency, amplitude, capacity, section_ratio):
    highest = lax.Precision.HIGHEST
    vectors = eigenvectors
    for panel in reversed(range(PANELS)):
        projection = jnp.dot(reflectors[panel].T, vectors, precision=highest)
        applied = jnp.dot(factors[panel], projection, precision=highest)
        vectors = vectors - jnp.dot(reflectors[panel], applied, precision=highest)
    weights_table = correlation(frequency).astype(jnp.float32)
    dof_blocks = jnp.moveaxis(dof_index.reshape(MEM_DOFS, N_ROW, MEM_DEV), 1, 0)
    stiff_blocks = jnp.moveaxis(stiffness.reshape(COMPS, MEM_DOFS, N_ROW, MEM_DEV), 2, 0)

    def one_block(inputs):
        dof_block, stiff_block = inputs
        picked = vectors[dof_block]
        member_force = jnp.einsum('cke,kem->cem', stiff_block, picked, precision=highest)
        scaled = (member_force * amplitude[None, None, :]).astype(jnp.bfloat16).astype(jnp.float32)
        weighted = jnp.einsum('cem,mn->cen', scaled, weights_table, precision=highest)
        return lax.optimization_barrier(jnp.sum(scaled * weighted, axis=-1))
    combined = lax.map(one_block, (dof_blocks, stiff_blocks))
    combined = jnp.moveaxis(combined, 0, 1).reshape(COMPS, MEMBERS)
    demand = combined / (capacity * capacity)
    resized = section_ratio * jnp.sqrt(0.25 + lax.optimization_barrier(jnp.sum(demand, axis=0)))
    return (vectors, demand, resized)
```

```python
import functools

import jax
import jax.numpy as jnp
from jax import lax
from jax.experimental import pallas as pl
from jax.experimental.pallas import tpu as pltpu
from jax.sharding import PartitionSpec as P

PANELS = 4
COLS = 256
HALO = 256
MEM_DOFS = 12
COMPS = 4
MODES = 1024
LANES = 128
bf16 = jnp.bfloat16
f32 = jnp.float32
VMEM_LIMIT = 58 * 1024 * 1024

damping_ratio = 0.05
PAIRS = (((0, 3), (1, 3), (2, 3)), ((0, 2), (1, 2), (0, 1)))


def contract_rows(a, b):
    return lax.dot_general(a, b, (((0,), (0,)), ((), ())), preferred_element_type=f32)


def mm(a, b):
    return jnp.dot(a, b, preferred_element_type=f32)


def project_kernel(core_ref, refl_ref, vec_ref, out_ref, half_ref, proj, gram):
    step = pl.program_id(0)

    @pl.when(step == 0)
    def _():
        proj[...] = jnp.zeros_like(proj)
        gram[...] = jnp.zeros_like(gram)

    vec = vec_ref[...].astype(bf16)
    half_ref[...] = vec
    refl = jnp.concatenate([refl_ref[p].astype(bf16) for p in range(PANELS)], axis=1)

    proj[...] += contract_rows(vec, refl)

    @pl.when(core_ref[0] == 0)
    def _():
        gram[...] += contract_rows(refl[:, 3 * COLS :], refl[:, : 3 * COLS])

    @pl.when(core_ref[0] == 1)
    def _():
        gram[:, : 2 * COLS] += contract_rows(refl[:, 2 * COLS : 3 * COLS], refl[:, : 2 * COLS])
        gram[:, 2 * COLS :] += contract_rows(refl[:, COLS : 2 * COLS], refl[:, :COLS])

    @pl.when(step == pl.num_programs(0) - 1)
    def _():
        rows = PANELS * COLS
        parts = proj.shape[0] // LANES
        for m in range(parts):
            out_ref[m * rows : (m + 1) * rows] = proj[m * LANES : (m + 1) * LANES].T.astype(bf16)
        start = parts * rows
        for m in range(COLS // LANES):
            out_ref[start : start + 3 * COLS] = gram[m * LANES : (m + 1) * LANES].T.astype(bf16)
            start += 3 * COLS


def project(core, reflectors, vectors):
    rows, cols = vectors.shape
    chunk = 512
    out_rows = (cols // LANES) * PANELS * COLS + (COLS // LANES) * 3 * COLS
    return pl.pallas_call(
        project_kernel,
        grid=(rows // chunk,),
        in_specs=[
            pl.BlockSpec(memory_space=pltpu.SMEM),
            pl.BlockSpec((PANELS, chunk, COLS), lambda i: (0, i, 0)),
            pl.BlockSpec((chunk, cols), lambda i: (i, 0)),
        ],
        out_specs=[
            pl.BlockSpec((out_rows, LANES), lambda i: (0, 0)),
            pl.BlockSpec((chunk, cols), lambda i: (i, 0)),
        ],
        out_shape=[
            jax.ShapeDtypeStruct((out_rows, LANES), bf16),
            jax.ShapeDtypeStruct((rows, cols), bf16),
        ],
        scratch_shapes=[pltpu.VMEM((cols, PANELS * COLS), f32), pltpu.VMEM((COLS, 3 * COLS), f32)],
        compiler_params=pltpu.CompilerParams(vmem_limit_bytes=VMEM_LIMIT),
        cost_estimate=pl.CostEstimate(flops=4 * rows * 256 * 512 * 4, bytes_accessed=14 << 20, transcendentals=0),
        name="project",
    )(core, reflectors, vectors)


def top_kernel(core_ref, vec_ref, refl_ref, out_ref):
    out_ref[:HALO] = vec_ref[...].astype(bf16)
    for h in range(2):
        out_ref[HALO:, h * COLS : (h + 1) * COLS] = refl_ref[2 * core_ref[0] + h].astype(bf16)


def top_rows(core, vectors, reflectors):
    cols = vectors.shape[1]
    return pl.pallas_call(
        top_kernel,
        grid=(1,),
        in_specs=[
            pl.BlockSpec(memory_space=pltpu.SMEM),
            pl.BlockSpec((HALO, cols), lambda i: (0, 0)),
            pl.BlockSpec((PANELS, HALO, COLS), lambda i: (0, 0, 0)),
        ],
        out_specs=pl.BlockSpec((2 * HALO, cols), lambda i: (0, 0)),
        out_shape=jax.ShapeDtypeStruct((2 * HALO, cols), bf16),
        name="top_rows",
    )(core, vectors, reflectors)


GROUP = 128
FILL = 1024
TERMS = COMPS * MEM_DOFS
AT_ONCE = 16


def lay_out(table, first, slot, block):
    table[pl.ds(first * 8 + slot, block.shape[0], stride=8), :] = block.astype(f32)


def strip(s):
    return slice(s * LANES, (s + 1) * LANES)


def spread_coefs(stiff_ref, wide):
    stiff = stiff_ref[...]
    high = stiff.astype(bf16)
    low = (stiff - high.astype(f32)).astype(bf16)
    both = jnp.concatenate([high, low], axis=1)
    lane = lax.broadcasted_iota(jnp.int32, (1, 2 * GROUP), 1) % GROUP
    ones = jnp.ones((2 * GROUP, LANES), bf16)
    for start in range(0, GROUP, AT_ONCE):
        picked = [
            both * jnp.where(lane == e, 1.0, 0.0).astype(bf16) for e in range(start, start + AT_ONCE)
        ]
        wide[start * TERMS : (start + AT_ONCE) * TERMS] = mm(jnp.concatenate(picked, axis=0), ones)


def member_rows(index_ref, stiff_ref, table, wide, sums, out_ref, step, members):
    spread_coefs(stiff_ref, wide)

    def one(i, _):
        e = step * GROUP + i
        stiff = wide[pl.ds(pl.multiple_of(i * TERMS, 8), TERMS), :]
        acc = [None] * COMPS
        for k in range(MEM_DOFS):
            at = pl.multiple_of(index_ref[k * members + e], 8)
            row = table[pl.ds(at, 8), :]
            for c in range(COMPS):
                j = c * MEM_DOFS + k
                term = stiff[j : j + 1] * row
                acc[c] = term if k == 0 else acc[c] + term
        for c in range(COMPS):
            sums[pl.ds(pl.multiple_of((c * GROUP + i) * 8, 8), 8), :] = acc[c]
        return 0

    lax.fori_loop(0, GROUP, one, 0, unroll=8)
    for c in range(COMPS):
        for s in range(8):
            out_ref[c, :, strip(s)] = sums[pl.ds(c * GROUP * 8 + s, GROUP, stride=8), :].astype(out_ref.dtype)


def refl_kernel(members, core_ref, index_ref, stiff_ref, refl_ref, halo_ref, end_ref, out_ref, flat_ref, table, wide, sums):
    step = pl.program_id(0)
    rows = table.shape[0] // 8 - HALO
    fills = rows // FILL

    @pl.when(step < fills)
    def _():
        for s in range(8):
            lay_out(table, step * FILL, s, refl_ref[s // 2, :, strip(s % 2)])
        for p in range(PANELS):
            flat_ref[:, p * COLS : (p + 1) * COLS] = refl_ref[p].astype(bf16)

    @pl.when(step == fills)
    def _():
        core = core_ref[0]
        for s in range(4):
            lay_out(table, rows, s + 4 * core, halo_ref[HALO:, strip(s)])
            lay_out(table, rows, s + 4 * (1 - core), end_ref[HALO : 2 * HALO, strip(s)])

    @pl.when(step >= fills)
    def _():
        member_rows(index_ref, stiff_ref, table, wide, sums, out_ref, step - fills, members)


def vec_kernel(members, core_ref, index_ref, stiff_ref, vec_ref, other_ref, halo_ref, end_ref, out_ref, table, wide, sums):
    step = pl.program_id(0)
    rows = table.shape[0] // 8 - HALO
    fills = rows // FILL

    @pl.when(step < fills)
    def _():
        for s in range(4):
            lay_out(table, step * FILL, s, vec_ref[:, strip(s)])
            lay_out(table, step * FILL, 4 + s, other_ref[:, strip(s)])

    @pl.when(step == fills)
    def _():
        for s in range(4):
            lay_out(table, rows, s, halo_ref[:HALO, strip(s)])
            lay_out(table, rows, 4 + s, end_ref[:HALO, strip(s)])

    @pl.when(step >= fills)
    def _():
        member_rows(index_ref, stiff_ref, table, wide, sums, out_ref, step - fills, members)


def gather(kernel, name, rows, core, index, stiff, blocks, block_specs, out_shape, flat=False):
    members = stiff.shape[1]
    fills = rows // FILL
    smem = pl.BlockSpec(memory_space=pltpu.SMEM)
    fill_at = lambda i: jnp.minimum(i, fills - 1)
    group_at = lambda i: jnp.maximum(i - fills, 0)
    whole = lambda i: (0, 0)
    out_specs = [pl.BlockSpec((COMPS, GROUP, MODES), lambda i: (0, group_at(i), 0))]
    if flat:
        out_specs.append(pl.BlockSpec((FILL, MODES), lambda i: (fill_at(i), 0)))
    return pl.pallas_call(
        functools.partial(kernel, members),
        grid=(fills + members // GROUP,),
        in_specs=[smem, smem, pl.BlockSpec((TERMS, GROUP), lambda i: (0, group_at(i)))]
        + [spec(fill_at) for spec in block_specs]
        + [pl.BlockSpec((2 * HALO, MODES // 2), whole), pl.BlockSpec((2 * HALO + 16, MODES // 2), whole)],
        out_specs=out_specs,
        out_shape=out_shape,
        scratch_shapes=[
            pltpu.VMEM(((rows + HALO) * 8, LANES), f32),
            pltpu.VMEM((TERMS * GROUP, LANES), f32),
            pltpu.VMEM((COMPS * GROUP * 8, LANES), f32),
        ],
        compiler_params=pltpu.CompilerParams(vmem_limit_bytes=VMEM_LIMIT),
        cost_estimate=pl.CostEstimate(flops=1 << 20, bytes_accessed=1 << 20, transcendentals=0),
        name=name,
    )(core, index, stiff, *blocks)


def gather_reflectors(core, index, stiff, reflectors, halo, end):
    rows = reflectors.shape[1]
    return gather(
        refl_kernel,
        "gather_reflectors",
        rows,
        core,
        index,
        stiff,
        (reflectors, halo, end),
        [lambda at: pl.BlockSpec((PANELS, FILL, COLS), lambda i: (0, at(i), 0))],
        [
            jax.ShapeDtypeStruct((COMPS, stiff.shape[1], MODES), bf16),
            jax.ShapeDtypeStruct((rows, MODES), bf16),
        ],
        flat=True,
    )


def gather_vectors(core, index, stiff, vectors, other, halo, end):
    rows, cols = vectors.shape
    spec = lambda at: pl.BlockSpec((FILL, cols), lambda i: (at(i), 0))
    return gather(
        vec_kernel,
        "gather_vectors",
        rows,
        core,
        index,
        stiff,
        (vectors, other, halo, end),
        [spec, spec],
        [jax.ShapeDtypeStruct((COMPS, stiff.shape[1], MODES), f32)],
    )[0]


def solve_panels(first, second, mine_ref, other_ref, factor_ref, coef):
    rows = PANELS * COLS
    parts = coef.shape[1] // 2 // LANES
    blocks = {}
    for ref, pairs in ((first, PAIRS[0]), (second, PAIRS[1])):
        for i, pair in enumerate(pairs):
            start = parts * rows + i * COLS
            blocks[pair] = jnp.concatenate(
                [ref[start : start + COLS], ref[start + 3 * COLS : start + 4 * COLS]], axis=1
            )
    for p in reversed(range(PANELS)):
        factor = factor_ref[p]
        high = factor.astype(bf16)
        low = (factor - high.astype(f32)).astype(bf16)
        now = jnp.concatenate(
            [
                ref[m * rows + p * COLS : m * rows + (p + 1) * COLS]
                for ref in (mine_ref, other_ref)
                for m in range(parts)
            ],
            axis=1,
        ).astype(f32)
        if p < PANELS - 1:
            gram = jnp.concatenate([blocks[(p, q)] for q in range(p + 1, PANELS)], axis=1)
            now = now - mm(gram, coef[(p + 1) * COLS :])
        now_high = now.astype(bf16)
        now_low = (now - now_high.astype(f32)).astype(bf16)
        coef[p * COLS : (p + 1) * COLS] = (
            mm(high, now_high) + (mm(low, now_high) + mm(high, now_low))
        ).astype(bf16)


def finish_kernel(
    core_ref, mine_ref, other_ref, factor_ref, vec_ref, flat_ref, force_ref, refl_ref, weight_ref, amp_ref,
    cap_ref, ratio_ref, out_ref, demand_ref, resized_ref, coef,
):
    step = pl.program_id(0)
    for core in range(2):

        @pl.when((step == 0) & (core_ref[0] == core))
        def _():
            pair = (mine_ref, other_ref) if core == 0 else (other_ref, mine_ref)
            solve_panels(*pair, mine_ref, other_ref, factor_ref, coef)

    @pl.when(step > 0)
    def _():
        group = force_ref.shape[1]
        force = force_ref[...].reshape(COMPS * group, MODES)
        force = force - mm(refl_ref[...].reshape(COMPS * group, MODES), coef[...])
        scaled = (force * amp_ref[...]).astype(bf16)
        part = None
        for b in range(MODES // COLS):
            upto = (b + 1) * COLS
            here = slice(b * COLS, upto)
            weighted = mm(scaled[:, here], weight_ref[here, here])
            if b > 0:
                weighted = weighted + 2.0 * mm(scaled[:, : b * COLS], weight_ref[: b * COLS, here])
            product = weighted * scaled[:, b * COLS : upto].astype(f32)
            both = product[:, :LANES] + product[:, LANES:]
            part = both if part is None else part + both
        total = jnp.full((1, group), 0.25, f32)
        for c in range(COMPS):
            combined = jnp.sum(part[c * group : (c + 1) * group].T, axis=0, keepdims=True)
            capacity = cap_ref[c : c + 1]
            demand = combined / (capacity * capacity)
            demand_ref[c : c + 1] = demand
            total = total + demand
        resized_ref[...] = ratio_ref[...] * jnp.sqrt(total)
        out_ref[...] = vec_ref[...] - mm(flat_ref[...], coef[:, : out_ref.shape[1]])


def finish(core, mine, other, factors, vectors, flat, from_vec, from_refl, weights, amp, capacity, ratio):
    members = from_vec.shape[1]
    rows, cols = vectors.shape
    group = 128
    steps = members // group
    chunk = rows // steps
    whole = pl.BlockSpec(memory_space=pltpu.VMEM)
    at = lambda i: jnp.maximum(i - 1, 0)
    return pl.pallas_call(
        finish_kernel,
        grid=(1 + steps,),
        in_specs=[
            pl.BlockSpec(memory_space=pltpu.SMEM),
            whole,
            whole,
            whole,
            pl.BlockSpec((chunk, cols), lambda i: (at(i), 0)),
            pl.BlockSpec((chunk, MODES), lambda i: (at(i), 0)),
            pl.BlockSpec((COMPS, group, MODES), lambda i: (0, at(i), 0)),
            pl.BlockSpec((COMPS, group, MODES), lambda i: (0, at(i), 0)),
            whole,
            whole,
            pl.BlockSpec((COMPS, group), lambda i: (0, at(i))),
            pl.BlockSpec((1, group), lambda i: (0, at(i))),
        ],
        out_specs=[
            pl.BlockSpec((chunk, cols), lambda i: (at(i), 0)),
            pl.BlockSpec((COMPS, group), lambda i: (0, at(i))),
            pl.BlockSpec((1, group), lambda i: (0, at(i))),
        ],
        out_shape=[
            jax.ShapeDtypeStruct((rows, cols), f32),
            jax.ShapeDtypeStruct((COMPS, members), f32),
            jax.ShapeDtypeStruct((1, members), f32),
        ],
        scratch_shapes=[pltpu.VMEM((PANELS * COLS, MODES), bf16)],
        compiler_params=pltpu.CompilerParams(vmem_limit_bytes=VMEM_LIMIT),
        cost_estimate=pl.CostEstimate(flops=12 << 30, bytes_accessed=30 << 20, transcendentals=0),
        name="finish",
    )(core, mine, other, factors, vectors, flat, from_vec, from_refl, weights, amp, capacity, ratio)


def correlation(frequency):
    freq_ratio = frequency[None, :] / frequency[:, None]
    squared = damping_ratio * damping_ratio
    numerator = 8.0 * squared * (1.0 + freq_ratio) * freq_ratio * jnp.sqrt(freq_ratio)
    denominator = (1.0 - freq_ratio * freq_ratio) ** 2 + 4.0 * squared * freq_ratio * (
        1.0 + freq_ratio
    ) ** 2
    return (numerator / denominator).astype(bf16)


def shards(
    eigenvectors,
    reflectors,
    factors,
    dof_index,
    stiffness,
    frequency,
    amplitude,
    capacity,
    section_ratio,
):
    row_count = lax.axis_size("row")
    core = lax.axis_index("mode")
    core_arr = core.astype(jnp.int32).reshape(1)
    rows, cols = eigenvectors.shape
    members = capacity.shape[1]
    swap = [(0, 1), (1, 0)]

    top = top_rows(core_arr, eigenvectors, reflectors)
    halo = lax.ppermute(top, "row", [(i + 1, i) for i in range(row_count - 1)])
    _, reflectors_after = lax.optimization_barrier((top, reflectors))
    partial_sums, half = project(core_arr, reflectors_after, eigenvectors)
    partial_sums, halo = lax.optimization_barrier((partial_sums, halo))
    shard = partial_sums.shape[0] // row_count
    pieces = lax.all_to_all(
        partial_sums.reshape(row_count, shard, LANES), "row", split_axis=0, concat_axis=0, tiled=True
    )

    other = lax.ppermute(half, "mode", swap)
    amp_high = amplitude.astype(bf16)
    amp_rest = amplitude - amp_high.astype(f32)
    amp_mid = amp_rest.astype(bf16)
    amp_low = (amp_rest - amp_mid.astype(f32)).astype(bf16)
    amp_rows = jnp.concatenate(
        [amp_high[None], amp_mid[None], amp_low[None], jnp.zeros((13, cols), bf16)], axis=0
    )
    end = lax.ppermute(jnp.concatenate([halo, amp_rows], axis=0), "mode", swap)
    amp_other = jnp.sum(end[2 * HALO : 2 * HALO + 3].astype(f32), axis=0)
    amp_all = jnp.concatenate([amplitude, amp_other])[None]

    first_row = lax.axis_index("row") * rows
    index = lax.dynamic_slice_in_dim(dof_index, core * members, members, axis=1)
    index = ((index - first_row) * 8).reshape(-1)
    stiff = lax.dynamic_slice_in_dim(stiffness, core * members, members, axis=2)
    stiff = stiff.reshape(TERMS, members)
    from_refl, flat = gather_reflectors(core_arr, index, stiff, reflectors, halo, end)
    pieces, from_refl, flat = lax.optimization_barrier((pieces, from_refl, flat))
    summed = jnp.sum(pieces.astype(f32), axis=0).astype(bf16)
    summed, frequency, index = lax.optimization_barrier((summed, frequency, index))
    spread = lax.all_to_all(
        jnp.broadcast_to(summed[None], (row_count, shard, LANES)), "row", split_axis=0, concat_axis=0, tiled=True
    )
    from_vec = gather_vectors(core_arr, index, stiff, eigenvectors, other, halo, end)

    freq_halves = frequency.reshape(2, cols)
    freq_all = jnp.where(core == 0, freq_halves, freq_halves[::-1]).reshape(-1)
    weights_table = correlation(freq_all)

    spread, from_vec, weights_table = lax.optimization_barrier((spread, from_vec, weights_table))
    sums_mine = spread.reshape(row_count * shard, LANES)
    sums_other = lax.ppermute(sums_mine, "mode", swap)
    vectors, demand, resized = finish(
        core_arr, sums_mine, sums_other, factors, eigenvectors, flat, from_vec, from_refl, weights_table,
        amp_all, capacity, section_ratio[None],
    )
    return (vectors, demand, resized.reshape(-1))


def solution(mesh):
    in_specs = (
        P("row", "mode"),
        P(None, "row", None),
        P(),
        P(None, "row"),
        P(None, None, "row"),
        P(),
        P("mode"),
        P(None, ("row", "mode")),
        P(("row", "mode")),
    )
    out_specs = (P("row", "mode"), P(None, ("row", "mode")), P(("row", "mode")))
    return jax.shard_map(shards, mesh=mesh, in_specs=in_specs, out_specs=out_specs, check_vma=False)
```

```python
import functools

import jax
import jax.numpy as jnp
from jax import lax
from jax.experimental import pallas as pl
from jax.experimental.pallas import tpu as pltpu
from jax.sharding import PartitionSpec as P

PANELS = 4
COLS = 256
HALO = 256
MEM_DOFS = 12
COMPS = 4
MODES = 1024
LANES = 128
bf16 = jnp.bfloat16
f32 = jnp.float32
MIB = 1024 * 1024

damping_ratio = 0.05
PAIRS = (((0, 3), (1, 3), (2, 3)), ((0, 2), (1, 2), (0, 1)))


def contract_rows(a, b):
    return lax.dot_general(a, b, (((0,), (0,)), ((), ())), preferred_element_type=f32)


def mm(a, b):
    return jnp.dot(a, b, preferred_element_type=f32)


def project_kernel(core_ref, refl_ref, vec_ref, out_ref, half_ref, proj, gram):
    step = pl.program_id(0)

    @pl.when(step == 0)
    def _():
        proj[...] = jnp.zeros_like(proj)
        gram[...] = jnp.zeros_like(gram)

    vec = vec_ref[...].astype(bf16)
    half_ref[...] = vec
    refl = jnp.concatenate([refl_ref[p].astype(bf16) for p in range(PANELS)], axis=1)

    proj[...] += contract_rows(vec, refl)

    @pl.when(core_ref[0] == 0)
    def _():
        gram[...] += contract_rows(refl[:, 3 * COLS :], refl[:, : 3 * COLS])

    @pl.when(core_ref[0] == 1)
    def _():
        gram[:, : 2 * COLS] += contract_rows(refl[:, 2 * COLS : 3 * COLS], refl[:, : 2 * COLS])
        gram[:, 2 * COLS :] += contract_rows(refl[:, COLS : 2 * COLS], refl[:, :COLS])

    @pl.when(step == pl.num_programs(0) - 1)
    def _():
        rows = PANELS * COLS
        parts = proj.shape[0] // LANES
        for m in range(parts):
            out_ref[m * rows : (m + 1) * rows] = proj[m * LANES : (m + 1) * LANES].T.astype(bf16)
        start = parts * rows
        for m in range(COLS // LANES):
            out_ref[start : start + 3 * COLS] = gram[m * LANES : (m + 1) * LANES].T.astype(bf16)
            start += 3 * COLS


def project(core, reflectors, vectors):
    rows, cols = vectors.shape
    chunk = 512
    out_rows = (cols // LANES) * PANELS * COLS + (COLS // LANES) * 3 * COLS
    return pl.pallas_call(
        project_kernel,
        grid=(rows // chunk,),
        in_specs=[
            pl.BlockSpec(memory_space=pltpu.SMEM),
            pl.BlockSpec((PANELS, chunk, COLS), lambda i: (0, i, 0)),
            pl.BlockSpec((chunk, cols), lambda i: (i, 0)),
        ],
        out_specs=[
            pl.BlockSpec((out_rows, LANES), lambda i: (0, 0)),
            pl.BlockSpec((chunk, cols), lambda i: (i, 0)),
        ],
        out_shape=[
            jax.ShapeDtypeStruct((out_rows, LANES), bf16),
            jax.ShapeDtypeStruct((rows, cols), bf16),
        ],
        scratch_shapes=[pltpu.VMEM((cols, PANELS * COLS), f32), pltpu.VMEM((COLS, 3 * COLS), f32)],
        compiler_params=pltpu.CompilerParams(vmem_limit_bytes=58 * MIB),
        cost_estimate=pl.CostEstimate(flops=4 * rows * 256 * 512 * 4, bytes_accessed=14 << 20, transcendentals=0),
        name="project",
    )(core, reflectors, vectors)


def top_kernel(core_ref, vec_ref, refl_ref, out_ref):
    out_ref[:HALO] = vec_ref[...].astype(bf16)
    for h in range(2):
        out_ref[HALO:, h * COLS : (h + 1) * COLS] = refl_ref[2 * core_ref[0] + h].astype(bf16)


def top_rows(core, vectors, reflectors):
    cols = vectors.shape[1]
    return pl.pallas_call(
        top_kernel,
        grid=(1,),
        in_specs=[
            pl.BlockSpec(memory_space=pltpu.SMEM),
            pl.BlockSpec((HALO, cols), lambda i: (0, 0)),
            pl.BlockSpec((PANELS, HALO, COLS), lambda i: (0, 0, 0)),
        ],
        out_specs=pl.BlockSpec((2 * HALO, cols), lambda i: (0, 0)),
        out_shape=jax.ShapeDtypeStruct((2 * HALO, cols), bf16),
        compiler_params=pltpu.CompilerParams(vmem_limit_bytes=58 * MIB),
        name="top_rows",
    )(core, vectors, reflectors)


GROUP = 128
FILL = 1024
TERMS = COMPS * MEM_DOFS
AT_ONCE = 16


def lay_out(table, first, slot, block):
    table[pl.ds(first * 8 + slot, block.shape[0], stride=8), :] = block.astype(f32)


def strip(s):
    return slice(s * LANES, (s + 1) * LANES)


def spread_coefs(stiff_ref, wide, group):
    stiff = stiff_ref[:, pl.ds(pl.multiple_of(group * GROUP, GROUP), GROUP)]
    base = group * GROUP * TERMS
    high = stiff.astype(bf16)
    low = (stiff - high.astype(f32)).astype(bf16)
    both = jnp.concatenate([high, low], axis=1)
    pair = lax.broadcasted_iota(jnp.int32, (1, 2 * GROUP), 1) % GROUP // 2
    odd = lax.broadcasted_iota(jnp.int32, (2 * GROUP, 2 * LANES), 0) % 2
    right = lax.broadcasted_iota(jnp.int32, (2 * GROUP, 2 * LANES), 1) // LANES
    select = jnp.where(odd == right, 1.0, 0.0).astype(bf16)
    for start in range(0, GROUP // 2, AT_ONCE):
        picked = [
            both * jnp.where(pair == e, 1.0, 0.0).astype(bf16) for e in range(start, start + AT_ONCE)
        ]
        spread = mm(jnp.concatenate(picked, axis=0), select)
        for t in range(AT_ONCE):
            for h in range(2):
                at = (2 * (start + t) + h) * TERMS
                wide[pl.ds(pl.multiple_of(base + at, 8), TERMS), :] = spread[t * TERMS : (t + 1) * TERMS, strip(h)]


def member_rows(index_ref, table, wide, sums, out_ref, step, members):
    def one(i, _):
        e = step * GROUP + i
        stiff = wide[pl.ds(pl.multiple_of(e * TERMS, 8), TERMS), :]
        acc = [None] * COMPS
        for k in range(MEM_DOFS):
            at = pl.multiple_of(index_ref[k * members + e], 8)
            row = table[pl.ds(at, 8), :]
            for c in range(COMPS):
                j = c * MEM_DOFS + k
                term = stiff[j : j + 1] * row
                acc[c] = term if k == 0 else acc[c] + term
        for c in range(COMPS):
            sums[pl.ds(pl.multiple_of((c * GROUP + i) * 8, 8), 8), :] = acc[c]
        return 0

    lax.fori_loop(0, GROUP, one, 0, unroll=8)
    for c in range(COMPS):
        for s in range(8):
            out_ref[c, :, strip(s)] = sums[pl.ds(c * GROUP * 8 + s, GROUP, stride=8), :].astype(out_ref.dtype)


def refl_kernel(members, core_ref, index_ref, stiff_ref, refl_ref, halo_ref, end_ref, out_ref, flat_ref, table, wide, sums):
    step = pl.program_id(0)
    rows = table.shape[0] // 8 - HALO
    fills = rows // FILL

    @pl.when(step < fills)
    def _():
        share = members // GROUP // fills
        for g in range(share):
            spread_coefs(stiff_ref, wide, step * share + g)
        for s in range(8):
            lay_out(table, step * FILL, s, refl_ref[s // 2, :, strip(s % 2)])
        for p in range(PANELS):
            flat_ref[:, p * COLS : (p + 1) * COLS] = refl_ref[p].astype(bf16)

    @pl.when(step == fills)
    def _():
        core = core_ref[0]
        for s in range(4):
            lay_out(table, rows, s + 4 * core, halo_ref[HALO:, strip(s)])
            lay_out(table, rows, s + 4 * (1 - core), end_ref[HALO : 2 * HALO, strip(s)])

    @pl.when(step >= fills)
    def _():
        member_rows(index_ref, table, wide, sums, out_ref, step - fills, members)


def vec_kernel(members, core_ref, index_ref, stiff_ref, vec_ref, other_ref, halo_ref, end_ref, out_ref, table, wide, sums):
    step = pl.program_id(0)
    rows = table.shape[0] // 8 - HALO
    fills = rows // FILL

    @pl.when(step < fills)
    def _():
        share = members // GROUP // fills
        for g in range(share):
            spread_coefs(stiff_ref, wide, step * share + g)
        for s in range(4):
            lay_out(table, step * FILL, s, vec_ref[:, strip(s)])
            lay_out(table, step * FILL, 4 + s, other_ref[:, strip(s)])

    @pl.when(step == fills)
    def _():
        for s in range(4):
            lay_out(table, rows, s, halo_ref[:HALO, strip(s)])
            lay_out(table, rows, 4 + s, end_ref[:HALO, strip(s)])

    @pl.when(step >= fills)
    def _():
        member_rows(index_ref, table, wide, sums, out_ref, step - fills, members)


def gather(kernel, name, rows, core, index, stiff, blocks, block_specs, out_shape, flat=False):
    members = stiff.shape[1]
    fills = rows // FILL
    smem = pl.BlockSpec(memory_space=pltpu.SMEM)
    fill_at = lambda i: jnp.minimum(i, fills - 1)
    group_at = lambda i: jnp.maximum(i - fills, 0)
    whole = lambda i: (0, 0)
    out_specs = [pl.BlockSpec((COMPS, GROUP, MODES), lambda i: (0, group_at(i), 0))]
    if flat:
        out_specs.append(pl.BlockSpec((FILL, MODES), lambda i: (fill_at(i), 0)))
    return pl.pallas_call(
        functools.partial(kernel, members),
        grid=(fills + members // GROUP,),
        in_specs=[smem, smem, pl.BlockSpec((TERMS, members), whole)]
        + [spec(fill_at) for spec in block_specs]
        + [pl.BlockSpec((2 * HALO, MODES // 2), whole), pl.BlockSpec((2 * HALO + 16, MODES // 2), whole)],
        out_specs=out_specs,
        out_shape=out_shape,
        scratch_shapes=[
            pltpu.VMEM(((rows + HALO) * 8, LANES), f32),
            pltpu.VMEM((TERMS * members, LANES), f32),
            pltpu.VMEM((COMPS * GROUP * 8, LANES), f32),
        ],
        compiler_params=pltpu.CompilerParams(vmem_limit_bytes=58 * MIB),
        cost_estimate=pl.CostEstimate(flops=1 << 20, bytes_accessed=1 << 20, transcendentals=0),
        name=name,
    )(core, index, stiff, *blocks)


def gather_reflectors(core, index, stiff, reflectors, halo, end):
    rows = reflectors.shape[1]
    return gather(
        refl_kernel,
        "gather_reflectors",
        rows,
        core,
        index,
        stiff,
        (reflectors, halo, end),
        [lambda at: pl.BlockSpec((PANELS, FILL, COLS), lambda i: (0, at(i), 0))],
        [
            jax.ShapeDtypeStruct((COMPS, stiff.shape[1], MODES), bf16),
            jax.ShapeDtypeStruct((rows, MODES), bf16),
        ],
        flat=True,
    )


def gather_vectors(core, index, stiff, vectors, other, halo, end):
    rows, cols = vectors.shape
    spec = lambda at: pl.BlockSpec((FILL, cols), lambda i: (at(i), 0))
    return gather(
        vec_kernel,
        "gather_vectors",
        rows,
        core,
        index,
        stiff,
        (vectors, other, halo, end),
        [spec, spec],
        [jax.ShapeDtypeStruct((COMPS, stiff.shape[1], MODES), f32)],
    )[0]


def solve_panels(first, second, mine_ref, other_ref, factor_ref, coef):
    rows = PANELS * COLS
    parts = coef.shape[1] // 2 // LANES
    blocks = {}
    for ref, pairs in ((first, PAIRS[0]), (second, PAIRS[1])):
        for i, pair in enumerate(pairs):
            start = parts * rows + i * COLS
            blocks[pair] = jnp.concatenate(
                [ref[start : start + COLS], ref[start + 3 * COLS : start + 4 * COLS]], axis=1
            )
    for p in reversed(range(PANELS)):
        factor = factor_ref[p]
        high = factor.astype(bf16)
        low = (factor - high.astype(f32)).astype(bf16)
        now = jnp.concatenate(
            [
                ref[m * rows + p * COLS : m * rows + (p + 1) * COLS]
                for ref in (mine_ref, other_ref)
                for m in range(parts)
            ],
            axis=1,
        ).astype(f32)
        if p < PANELS - 1:
            gram = jnp.concatenate([blocks[(p, q)] for q in range(p + 1, PANELS)], axis=1)
            now = now - mm(gram, coef[(p + 1) * COLS :])
        now_high = now.astype(bf16)
        now_low = (now - now_high.astype(f32)).astype(bf16)
        coef[p * COLS : (p + 1) * COLS] = (
            mm(high, now_high) + (mm(low, now_high) + mm(high, now_low))
        ).astype(bf16)


def finish_kernel(
    steps, core_ref, mine_ref, other_ref, factor_ref, vec_hbm, flat_hbm, force_hbm, refl_hbm, weight_hbm, amp_ref,
    cap_ref, ratio_ref, out_hbm, demand_ref, resized_ref, coef, vec_buf, flat_buf, force_buf, refl_buf, weight_ref,
    out_buf, in_sems, out_sems, weight_sem,
):
    chunk = vec_buf.shape[1]
    group = force_buf.shape[2]

    def copies(i):
        slot = i % 2
        rows = pl.ds(i * chunk, chunk)
        found = pl.ds(i * group, group)
        return [
            pltpu.make_async_copy(refl_hbm.at[:, found], refl_buf.at[slot], in_sems.at[slot, 0]),
            pltpu.make_async_copy(force_hbm.at[:, found], force_buf.at[slot], in_sems.at[slot, 1]),
            pltpu.make_async_copy(flat_hbm.at[rows], flat_buf.at[slot], in_sems.at[slot, 2]),
            pltpu.make_async_copy(vec_hbm.at[rows], vec_buf.at[slot], in_sems.at[slot, 3]),
        ]

    weight_copy = pltpu.make_async_copy(weight_hbm, weight_ref, weight_sem)
    for i in range(2):
        for copy in copies(i):
            copy.start()
        if i == 0:
            weight_copy.start()

    for core in range(2):

        @pl.when(core_ref[0] == core)
        def _():
            pair = (mine_ref, other_ref) if core == 0 else (other_ref, mine_ref)
            solve_panels(*pair, mine_ref, other_ref, factor_ref, coef)

    out_copies = []
    for i in range(steps):
        slot = i % 2
        refl_copy, force_copy, flat_copy, vec_copy = copies(i)
        refl_copy.wait()
        force_copy.wait()
        if i == 0:
            weight_copy.wait()
        force = force_buf[slot].reshape(COMPS * group, MODES)
        force = force - mm(refl_buf[slot].reshape(COMPS * group, MODES), coef[...])
        scaled = (force * amp_ref[...]).astype(bf16)
        part = None
        for b in range(MODES // COLS):
            upto = (b + 1) * COLS
            here = slice(b * COLS, upto)
            weighted = mm(scaled[:, here], weight_ref[here, here])
            if b > 0:
                weighted = weighted + 2.0 * mm(scaled[:, : b * COLS], weight_ref[: b * COLS, here])
            product = weighted * scaled[:, here].astype(f32)
            both = product[:, :LANES] + product[:, LANES:]
            part = both if part is None else part + both
        along = slice(i * group, (i + 1) * group)
        total = jnp.full((1, group), 0.25, f32)
        for c in range(COMPS):
            combined = jnp.sum(part[c * group : (c + 1) * group].T, axis=0, keepdims=True)
            capacity = cap_ref[c : c + 1, along]
            demand = combined / (capacity * capacity)
            demand_ref[c : c + 1, along] = demand
            total = total + demand
        resized_ref[:, along] = ratio_ref[:, along] * jnp.sqrt(total)
        flat_copy.wait()
        vec_copy.wait()
        if i >= 2:
            out_copies[i - 2].wait()
        out_buf[slot] = vec_buf[slot] - mm(flat_buf[slot], coef[:, : out_buf.shape[2]])
        out_copy = pltpu.make_async_copy(out_buf.at[slot], out_hbm.at[pl.ds(i * chunk, chunk)], out_sems.at[slot])
        out_copy.start()
        out_copies.append(out_copy)
        if i + 2 < steps:
            for copy in copies(i + 2):
                copy.start()
    for out_copy in out_copies[-2:]:
        out_copy.wait()


def finish(core, mine, other, factors, vectors, flat, from_vec, from_refl, weights, amp, capacity, ratio):
    members = from_vec.shape[1]
    rows, cols = vectors.shape
    group = 128
    steps = members // group
    chunk = rows // steps
    here = pl.BlockSpec(memory_space=pltpu.VMEM)
    there = pl.BlockSpec(memory_space=pl.ANY)
    return pl.pallas_call(
        functools.partial(finish_kernel, steps),
        in_specs=[pl.BlockSpec(memory_space=pltpu.SMEM), here, here, here]
        + [there] * 5
        + [here] * 3,
        out_specs=[there, here, here],
        out_shape=[
            jax.ShapeDtypeStruct((rows, cols), f32),
            jax.ShapeDtypeStruct((COMPS, members), f32),
            jax.ShapeDtypeStruct((1, members), f32),
        ],
        scratch_shapes=[
            pltpu.VMEM((PANELS * COLS, MODES), bf16),
            pltpu.VMEM((2, chunk, cols), f32),
            pltpu.VMEM((2, chunk, MODES), bf16),
            pltpu.VMEM((2, COMPS, group, MODES), f32),
            pltpu.VMEM((2, COMPS, group, MODES), bf16),
            pltpu.VMEM((MODES, MODES), bf16),
            pltpu.VMEM((2, chunk, cols), f32),
            pltpu.SemaphoreType.DMA((2, 4)),
            pltpu.SemaphoreType.DMA((2,)),
            pltpu.SemaphoreType.DMA,
        ],
        compiler_params=pltpu.CompilerParams(vmem_limit_bytes=58 * MIB),
        cost_estimate=pl.CostEstimate(flops=12 << 30, bytes_accessed=30 << 20, transcendentals=0),
        name="finish",
    )(core, mine, other, factors, vectors, flat, from_vec, from_refl, weights, amp, capacity, ratio)


def correlation(frequency):
    inverse = 1.0 / frequency
    root = jnp.sqrt(frequency)
    inverse_root = 1.0 / root
    squared = damping_ratio * damping_ratio
    ratio = frequency[None, :] * inverse[:, None]
    power = (frequency * root)[None, :] * (inverse * inverse_root)[:, None]
    above = 1.0 + ratio
    below = 1.0 - ratio
    numerator = (8.0 * squared) * above * power
    denominator = (above * above) * (below * below + (4.0 * squared) * ratio)
    return (numerator / denominator).astype(bf16)


def shards(
    eigenvectors,
    reflectors,
    factors,
    dof_index,
    stiffness,
    frequency,
    amplitude,
    capacity,
    section_ratio,
):
    row_count = lax.axis_size("row")
    core = lax.axis_index("mode")
    core_arr = core.astype(jnp.int32).reshape(1)
    rows, cols = eigenvectors.shape
    members = capacity.shape[1]
    swap = [(0, 1), (1, 0)]

    top = top_rows(core_arr, eigenvectors, reflectors)
    halo = lax.ppermute(top, "row", [(i + 1, i) for i in range(row_count - 1)])
    _, reflectors_after = lax.optimization_barrier((top, reflectors))
    partial_sums, half = project(core_arr, reflectors_after, eigenvectors)
    first_row = lax.axis_index("row") * rows
    index = lax.dynamic_slice_in_dim(dof_index, core * members, members, axis=1)
    index = ((index - first_row) * 8).reshape(-1)
    stiff = lax.dynamic_slice_in_dim(stiffness, core * members, members, axis=2)
    stiff = stiff.reshape(TERMS, members)
    partial_sums, halo, index, stiff = lax.optimization_barrier((partial_sums, halo, index, stiff))
    shard = partial_sums.shape[0] // row_count
    pieces = lax.all_to_all(
        partial_sums.reshape(row_count, shard, LANES), "row", split_axis=0, concat_axis=0, tiled=True
    )

    amp_high = amplitude.astype(bf16)
    amp_rest = amplitude - amp_high.astype(f32)
    amp_mid = amp_rest.astype(bf16)
    amp_low = (amp_rest - amp_mid.astype(f32)).astype(bf16)
    amp_rows = jnp.concatenate(
        [amp_high[None], amp_mid[None], amp_low[None], jnp.zeros((13, cols), bf16)], axis=0
    )
    end = lax.ppermute(jnp.concatenate([halo, amp_rows], axis=0), "mode", swap)
    end, half = lax.optimization_barrier((end, half))
    other = lax.ppermute(half, "mode", swap)
    amp_other = jnp.sum(end[2 * HALO : 2 * HALO + 3].astype(f32), axis=0)
    amp_all = jnp.concatenate([amplitude, amp_other])[None]

    from_refl, flat = gather_reflectors(core_arr, index, stiff, reflectors, halo, end)
    pieces, from_refl, flat = lax.optimization_barrier((pieces, from_refl, flat))
    summed = jnp.sum(pieces.astype(f32), axis=0).astype(bf16)
    summed, frequency, index = lax.optimization_barrier((summed, frequency, index))
    spread = lax.all_to_all(
        jnp.broadcast_to(summed[None], (row_count, shard, LANES)), "row", split_axis=0, concat_axis=0, tiled=True
    )
    from_vec = gather_vectors(core_arr, index, stiff, eigenvectors, other, halo, end)

    freq_halves = frequency.reshape(2, cols)
    freq_all = jnp.where(core == 0, freq_halves, freq_halves[::-1]).reshape(-1)
    weights_table = correlation(freq_all)

    spread, from_vec, weights_table = lax.optimization_barrier((spread, from_vec, weights_table))
    sums_mine = spread.reshape(row_count * shard, LANES)
    sums_other = lax.ppermute(sums_mine, "mode", swap)
    vectors, demand, resized = finish(
        core_arr, sums_mine, sums_other, factors, eigenvectors, flat, from_vec, from_refl, weights_table,
        amp_all, capacity, section_ratio[None],
    )
    return (vectors, demand, resized.reshape(-1))


def solution(mesh):
    in_specs = (
        P("row", "mode"),
        P(None, "row", None),
        P(),
        P(None, "row"),
        P(None, None, "row"),
        P(),
        P("mode"),
        P(None, ("row", "mode")),
        P(("row", "mode")),
    )
    out_specs = (P("row", "mode"), P(None, ("row", "mode")), P(("row", "mode")))
    return jax.shard_map(shards, mesh=mesh, in_specs=in_specs, out_specs=out_specs, check_vma=False)
```
